32 devices in a mesh: groups: 2 (over y), expert: 16 (over z, x, core), tensor: 1.
Axes of the slice: x: 2, y: 2, z: 4, core: 2. Of those that a mesh axis runs over, the one named last changes fastest.
Arguments:
- attn_part: bfloat16 [1, 2048, 3584], P('tensor', ('groups', 'expert')), parts along dimension 1, may hold values from -64 to 64
- resid: bfloat16 [2048, 3584], P(('groups', 'expert')), parts along dimension 0, may hold values from -6 to 6
- norm_gain: bfloat16 [3584], replicated, may hold values from 0.25 to 1.75
- routes: int32 [2048, 8], P(('groups', 'expert')), parts along dimension 0, may hold values from 0 to 15, all different within a row; in each aligned block of 64 rows (0 to 63, 64 to 127, ...) at most 64 rows name the same one
- gate_codes: int32 [2048, 8], P(('groups', 'expert')), parts along dimension 0, may hold values from 1 to 4095
- w_gate: bfloat16 [16, 3584, 1024], P('expert', None, 'tensor'), may hold values from -0.09375 to 0.09375
- w_up: bfloat16 [16, 3584, 1024], P('expert', None, 'tensor'), may hold values from -0.09375 to 0.09375
- w_down: bfloat16 [16, 1024, 3584], P('expert', 'tensor'), may hold values from -0.1875 to 0.1875
Outputs:
- moe_out: bfloat16 [2048, 3584], P(('groups', 'expert'), 'tensor'), parts along dimension 0
The draws below stay inside these ranges and needn't reach their ends.
There are 2 independent parts, one for each index of `groups`. The reference program is written for one: setup_inputs(seed, part) draws one part's arguments, and reference() takes and returns one part's arrays. A program takes and returns all parts, laid end to end along the dimension named above; an argument that names none is the same for every part. Nothing has to cross between parts.
Inputs may be any that keep to these rules, and one draw needn't show every extreme that they name: `routes`: each row names 8 different experts; among the rows of one device no expert is named by more than 64 rows, a bound that some block reaches.
All inputs are finite; a program needn't handle non-finite values.
Results may differ from the reference program's by a relative error of at most 0.035.
Values may be sent and summed in bfloat16 or wider, within the bound.
A program may use at most 192 MiB of HBM per device.

```python
import math
import jax
import jax.numpy as jnp
import numpy as np
from jax import lax

D = 3584
FF = 1024
TOP = 8
TOK_DEV = 64
TOKENS = 1024
EXPERTS = 16
CAP = 64
HEAD_GROUPS = 1
FF_BLOCK = 1024
N_EXPERT = 16
N_TENSOR = 1


def draw_attn_part(key, part):
    key = jax.random.fold_in(key, 11)
    k_row, k_col, k_base = jax.random.split(key, 3)
    row_scale = 10.0 ** jax.random.uniform(k_row, (1, TOKENS, 1), jnp.float32)
    col_trend = 10.0 ** (jnp.arange(D, dtype=jnp.float32) / D)
    col_scale = col_trend[None, None, :] * jnp.exp(jax.random.uniform(k_col, (1, 1, D), jnp.float32, -0.3, 0.3))
    values = jnp.clip(jax.random.normal(k_base, (HEAD_GROUPS, TOKENS, D), jnp.float32), -4.0, 4.0)
    scaled = values * row_scale * col_scale / 3.0
    return jnp.clip(scaled, -64.0, 64.0).astype(jnp.bfloat16)


def with_ends(values, own_key, smallest, top_value):
    spot = [jax.random.randint(jax.random.fold_in(own_key, axis), (), 0, length) for axis, length in enumerate(values.shape)]
    main_axis = values.shape.index(max(values.shape))
    neighbour = spot[:main_axis] + [(spot[main_axis] + 1) % values.shape[main_axis]] + spot[main_axis + 1:]
    return values.at[tuple(spot)].set(smallest).at[tuple(neighbour)].set(top_value)


def shard_levels(own_key, shape, shards, least, largest):
    def one(dim, blocks):
        steps = jax.random.uniform(jax.random.fold_in(jax.random.fold_in(own_key, 6), dim), (blocks,), jnp.float32, least / len(shards), largest / len(shards))
        return jnp.repeat(jnp.exp(steps), shape[dim] // blocks).reshape((-1,) + (1,) * (len(shape) - dim - 1))

    loudness = one(*shards[0])
    for cut in shards[1:]:
        loudness = loudness * one(*cut)
    return loudness


def routed_block(rng, own, number, rows, number_of, top, most, skew):
    order = jax.random.permutation(rng, number_of)
    packed, usual = shares(number_of, rows * top, most, skew, True), shares(number_of, rows * top, most, skew, False)
    places = jnp.arange(number_of)

    def named(lengths, offset_by):
        used = int((lengths > 0).sum())
        fixed = max(1, used // 4)
        shifted = fixed + (places - fixed + offset_by * (used - fixed)) % max(1, number_of - fixed)
        return jnp.zeros((number_of,), jnp.int32).at[order[jnp.where(places < fixed, places, shifted)]].set(jnp.asarray(lengths, jnp.int32))

    lengths = jnp.where(number % 4 == 0, named(packed, number // 4), named(usual, number - number // 4 - 1))
    mixed = jax.random.permutation(jax.random.fold_in(own, 3), number_of)
    giver, taker = mixed[0:number_of // 2 * 2:2], mixed[1:number_of // 2 * 2:2]
    room = jnp.minimum(lengths[giver] - 1, most - lengths[taker]) // 2
    room = jnp.where((giver == order[0]) | (taker == order[0]) | (lengths[taker] == 0), 0, jnp.maximum(room, 0))
    shifted = jax.random.randint(jax.random.fold_in(own, 4), (number_of // 2,), 0, 1 << 20) % (room + 1)
    lengths = lengths.at[giver].add(-shifted).at[taker].add(shifted)
    items = jnp.searchsorted(jnp.cumsum(lengths), jnp.arange(rows * top), side="right").astype(jnp.int32)
    grid = items.reshape(top, rows).T
    grid = grid[jax.random.permutation(jax.random.fold_in(own, 1), rows)]
    offset_by = jax.random.randint(jax.random.fold_in(own, 2), (rows, 1), 0, top)
    return jnp.take_along_axis(grid, (jnp.arange(top)[None, :] + offset_by) % top, axis=1)


def shares(amount, total, reach, slope, full):
    portions = [(1 << 20) // math.isqrt(grade ** slope) + 1 for grade in range(1, amount + 1)]
    largest = reach if full else min(reach, max(-(-total // amount), total * portions[0] // sum(portions)))
    least = 1 if total - largest >= amount - 1 else 0
    given, rest = [largest] + [least] * (amount - 1), total - largest - least * (amount - 1)
    while rest > 0:
        movable = [i for i in range(1, amount) if given[i] < largest] or [i for i in range(1, amount) if given[i] < reach]
        whole, remaining = sum([portions[i] for i in movable]), rest
        for i in movable:
            extra = min(reach - given[i], max(1, remaining * portions[i] // whole), rest)
            given[i] = given[i] + extra
            rest = rest - extra
    return np.array(given)


def scatter_about(rng, shape, width, reach, shards=(), kind=jnp.bfloat16):
    gain = shard_levels(rng, shape, shards, -0.22, 0.18) if shards else 1.0
    values = jax.random.normal(rng, shape, jnp.float32) * width * gain
    return jnp.minimum(jnp.maximum(values, -reach), reach).astype(kind)


def setup_inputs(seed: int = 0, part: int = 0) -> dict:
    splits = jax.random.split(jax.random.key(seed), 9)
    own_keys = jax.random.split(jax.random.fold_in(splits[8], part), 9)
    attn_part = draw_attn_part(jax.random.fold_in(jax.random.fold_in(splits[8], part), 71), part)
    resid = scatter_about(own_keys[1], (TOKENS, D), 1.0, 6.0, ((0, 16),))
    norm_gain = jnp.clip(1.0 + 0.15 * jax.random.normal(splits[2], (D,), jnp.float32), 0.25, 1.75).astype(jnp.bfloat16)
    routes_keys = jax.random.split(jax.random.fold_in(own_keys[3], 1), TOKENS // TOK_DEV)
    routes_turns = jax.random.permutation(jax.random.fold_in(own_keys[3], 3), TOKENS // TOK_DEV)
    routes = jax.vmap(lambda own, number: routed_block(jax.random.fold_in(own_keys[3], 2), own, number, TOK_DEV, EXPERTS, TOP, CAP, 2))(routes_keys, routes_turns).reshape((TOKENS, TOP))
    gate_codes = with_ends(jax.random.randint(own_keys[4], (TOKENS, TOP), 1, 4096), jax.random.fold_in(own_keys[4], 1), 1, 4095).astype(jnp.int32)
    w_gate = scatter_about(splits[5], (EXPERTS, D, FF), D ** -0.5, 0.09375, ((0, 16),))
    w_up = scatter_about(splits[6], (EXPERTS, D, FF), D ** -0.5, 0.09375, ((0, 16),))
    w_down = scatter_about(splits[7], (EXPERTS, FF, D), FF ** -0.5, 0.1875, ((0, 16),))
    return {"attn_part": attn_part, "resid": resid, "norm_gain": norm_gain, "routes": routes, "gate_codes": gate_codes, "w_gate": w_gate, "w_up": w_up, "w_down": w_down}


def reference(attn_part, resid, norm_gain, routes, gate_codes, w_gate, w_up, w_down):
    attn = lax.optimization_barrier(jnp.sum(attn_part.astype(jnp.float32), axis=0))
    stream = resid.astype(jnp.float32) + attn
    mean_sq = lax.optimization_barrier(jnp.mean(stream * stream, axis=1, keepdims=True))
    normed = (stream * lax.rsqrt(mean_sq + 1e-06) * norm_gain.astype(jnp.float32)).astype(jnp.bfloat16)
    codes = gate_codes.astype(jnp.float32)
    weights = codes / lax.optimization_barrier(jnp.sum(codes, axis=1, keepdims=True))
    flat_routes = routes.reshape(-1)
    flat_weights = weights.reshape(-1)
    limit = CAP * N_EXPERT

    def per_expert(total, expert):
        hit = flat_routes == expert
        index = jnp.nonzero(hit, size=limit, fill_value=0)[0].astype(jnp.int32)
        count = jnp.sum(hit.astype(jnp.int32))
        tok_index = (index // TOP).astype(jnp.int32)
        rows = normed[tok_index]
        gate = jnp.dot(rows, w_gate[expert], preferred_element_type=jnp.float32)
        up = jnp.dot(rows, w_up[expert], preferred_element_type=jnp.float32)
        hidden = (jax.nn.silu(gate) * up).astype(jnp.bfloat16)
        down = w_down[expert]
        summed = jnp.zeros((limit, D), jnp.float32)
        for block in range(N_TENSOR):
            lower = block * FF_BLOCK
            piece = jnp.dot(hidden[:, lower:lower + FF_BLOCK], down[lower:lower + FF_BLOCK], preferred_element_type=jnp.float32)
            summed = summed + lax.optimization_barrier(piece.astype(jnp.bfloat16)).astype(jnp.float32)
        valid = (jnp.arange(limit, dtype=jnp.int32) < count).astype(jnp.float32)
        coeffs = flat_weights[index] * valid
        total = total.at[tok_index].add(summed * coeffs[:, None])
        return (total, None)
    start = jnp.zeros((TOKENS, D), jnp.float32)
    total, unused = lax.scan(per_expert, start, jnp.arange(EXPERTS, dtype=jnp.int32))
    return total.astype(jnp.bfloat16)
```

```python
import functools

import jax
import jax.numpy as jnp
from jax import lax
from jax.experimental import pallas as pl
from jax.experimental.pallas import tpu as pltpu
from jax.sharding import PartitionSpec as P

UP_COLS = 256
DOWN_COLS = 512
LANES = 128


def ring_place(index, n):
    depth = n // 4
    core, x, z = index % 2, (index // 2) % 2, index // 4
    return 2 * (z + x * (2 * depth - 1 - 2 * z)) + core


def ring_index(place, n):
    depth = n // 4
    core, q = place % 2, place // 2
    x = q // depth
    z = q + x * (2 * depth - 1 - 2 * q)
    return (z * 2 + x) * 2 + core


def left_slot(d):
    return max(2 * d - 1, 0)


def right_slot(d, n):
    return n - 1 if d == n // 2 else 2 * d


def return_order(n):
    far = n // 2
    order = [(far - 1, 1), (far, 0), (far - 1, 0)]
    for d in range(far - 2, 0, -1):
        order += [(d, 1), (d, 0)]
    return order


def groups_of(n):
    far = n // 2
    found = [(0, 3, 1)]
    d = 2
    while d < far - 2:
        found.append((left_slot(d), 4, 2 * d + 1))
        d += 2
    while d < far:
        found.append((left_slot(d), 2, 2 * d - 1))
        d += 1
    found.append((n - 1, 1, n - 2))
    return found


def ring_kernel(
    n, attn, resid, gain, routes, codes, w_gate, w_up, w_down, out,
    rows, parts, back, shares, scale, hidden, v_gate, v_up, v_down,
    out_send, out_recv, share_send, share_recv, back_send, back_recv, load_sem,
):
    me = lax.axis_index("expert")
    place = ring_place(me, n)
    right = ring_index((place + 1) % n, n)
    left = ring_index((place + n - 1) % n, n)
    ways = ({"expert": right}, {"expert": left})
    tok = resid.shape[0]
    half = tok // 2
    experts_pad = shares.shape[1]

    barrier = pltpu.get_barrier_semaphore()
    for way in ways:
        pl.semaphore_signal(barrier, inc=1, device_id=way, device_id_type=pl.DeviceIdType.MESH)

    loads = [
        pltpu.make_async_copy(w_gate.at[0], v_gate, load_sem.at[0]),
        pltpu.make_async_copy(w_up.at[0], v_up, load_sem.at[1]),
        pltpu.make_async_copy(w_down.at[0], v_down, load_sem.at[2]),
    ]
    for load in loads:
        load.start()

    def norm(first, count):
        at = pl.ds(first, count)
        stream = resid[at, :].astype(jnp.float32) + attn[0, at, :].astype(jnp.float32)
        mean_sq = jnp.mean(stream * stream, axis=1, keepdims=True)
        scaled = stream * lax.rsqrt(mean_sq + 1e-06) * gain[...].astype(jnp.float32)
        rows[at, :] = scaled.astype(jnp.bfloat16)

    for first in range(0, tok, 16):
        norm(first, 16)

    code = codes[...].astype(jnp.float32)
    weight = code / jnp.sum(code, axis=1, keepdims=True)
    lane = lax.broadcasted_iota(jnp.int32, (tok, LANES), 1)
    dense = jnp.zeros((tok, LANES), jnp.float32)
    for k in range(routes.shape[1]):
        dense = dense + jnp.where(lane == routes[:, k:k + 1], weight[:, k:k + 1], 0.0)
    high = dense.astype(jnp.bfloat16).astype(jnp.float32)
    both = jnp.concatenate([high, dense - high], axis=0)
    shares[0] = both.T[:experts_pad].astype(jnp.bfloat16)

    pl.semaphore_wait(barrier, 2)

    def piece(slot, which):
        return pl.ds(slot * tok + which * half, half)

    def slot_of(way, d):
        return left_slot(d) if way == 0 else right_slot(d, n)

    def outward(way, j):
        d, which = j // 2, (j % 2 if way == 0 else 1 - j % 2)
        here, there = slot_of(way, d), slot_of(way, d + 1)
        return pltpu.make_async_remote_copy(
            rows.at[piece(here, which)], rows.at[piece(there, which)],
            out_send.at[way, j], out_recv.at[way, j],
            device_id=ways[way], device_id_type=pl.DeviceIdType.MESH,
        )

    def share(way, d):
        return pltpu.make_async_remote_copy(
            shares.at[slot_of(way, d)], shares.at[slot_of(way, d + 1)],
            share_send.at[way, d], share_recv.at[way, d],
            device_id=ways[way], device_id_type=pl.DeviceIdType.MESH,
        )

    def has_share(way, j):
        return j % 2 == 0 and not (way == 1 and j // 2 == n // 2 - 1)

    def send_out(way, j):
        if has_share(way, j):
            share(way, j // 2).start()
        outward(way, j).start()

    def arrive(j):
        for way in range(2):
            outward(way, j).wait_recv()
            if has_share(way, j):
                share(way, j // 2).wait_recv()
            if j + 2 < n - 1:
                send_out(way, j + 2)

    for j in range(2):
        for way in range(2):
            send_out(way, j)

    pick = (lax.broadcasted_iota(jnp.int32, (experts_pad, LANES), 0) == me).astype(jnp.bfloat16)

    def prepare(first, count):
        for slot in range(first, first + count):
            wide = lax.dot_general(
                shares[slot], pick, (((0,), (0,)), ((), ())), preferred_element_type=jnp.float32
            )
            scale[pl.ds(slot * tok, tok), :] = wide[:tok] + wide[tok:]

    def up_step(first, count, c):
        at = pl.ds(first * tok, count * tok)
        cols = pl.ds(pl.multiple_of(c * UP_COLS, UP_COLS), UP_COLS)
        x = rows[at, :]
        gate = jnp.dot(x, v_gate[:, cols], preferred_element_type=jnp.float32)
        up = jnp.dot(x, v_up[:, cols], preferred_element_type=jnp.float32)
        factor = jnp.concatenate([scale[at, :]] * (UP_COLS // LANES), axis=1)
        value = gate / (1.0 + jnp.exp(-gate)) * up * factor
        hidden[pl.ds(0, count * tok), cols] = value.astype(jnp.bfloat16)

    def down_step(first, count, c):
        cols = pl.ds(pl.multiple_of(c * DOWN_COLS, DOWN_COLS), DOWN_COLS)
        total = jnp.dot(
            hidden[pl.ds(0, count * tok), :], v_down[:, cols], preferred_element_type=jnp.float32
        )
        parts[pl.ds(first * tok, count * tok), cols] = total.astype(jnp.bfloat16)

    up_steps = v_gate.shape[1] // UP_COLS
    down_steps = v_down.shape[1] // DOWN_COLS
    up_cost = 2 * v_gate.shape[0] * UP_COLS
    down_cost = v_down.shape[0] * DOWN_COLS
    whole_cost = up_steps * up_cost + down_steps * down_cost

    def multiply(first, count, begin, end):
        def inside(done, cost):
            return begin <= (done + cost / 2) / whole_cost < end

        ups = [c for c in range(up_steps) if inside(c * up_cost, up_cost)]
        downs = [c for c in range(down_steps) if inside(up_steps * up_cost + c * down_cost, down_cost)]
        if ups:
            @pl.loop(ups[0], ups[-1] + 1)
            def _(c):
                up_step(first, count, c)
        if downs:
            @pl.loop(downs[0], downs[-1] + 1)
            def _(c):
                down_step(first, count, c)

    orders = return_order(n)

    def backward(way, j):
        d, which = orders[j]
        which = which if way == 0 else 1 - which
        slot = slot_of(1 - way, d)
        return pltpu.make_async_remote_copy(
            parts.at[piece(slot, which)], back.at[way, j],
            back_send.at[way, j], back_recv.at[way, j],
            device_id=ways[way], device_id_type=pl.DeviceIdType.MESH,
        )

    def send_back(way, j):
        d, which = orders[j]
        if (d + 1, which) in orders:
            earlier = orders.index((d + 1, which))
            backward(way, earlier).wait_recv()
            at = piece(slot_of(1 - way, d), which if way == 0 else 1 - which)
            total = parts[at, :].astype(jnp.float32) + back[way, earlier].astype(jnp.float32)
            parts[at, :] = total.astype(jnp.bfloat16)
        backward(way, j).start()

    plan = groups_of(n)
    arrived = -1
    for g, (first, count, needed) in enumerate(plan):
        while arrived < needed:
            arrived += 1
            arrive(arrived)
        if g == 0:
            for load in loads:
                load.wait()
        prepare(first, count)
        later = plan[g + 1][2] if g + 1 < len(plan) else arrived
        gaps = max(later - arrived, 1)
        for gap in range(gaps):
            multiply(first, count, gap / gaps, (gap + 1) / gaps if gap + 1 < gaps else 2.0)
            if gap + 1 < gaps:
                arrived += 1
                arrive(arrived)
        if g == len(plan) - 2:
            for way in range(2):
                send_back(way, 0)

    for j in range(1, n - 1):
        for way in range(2):
            send_back(way, j)

    for k in range(2):
        which = 1 - k
        at = pl.ds(which * half, half)
        total = parts[at, :].astype(jnp.float32)
        for way in range(2):
            j = orders.index((1, which if way == 0 else 1 - which))
            backward(way, j).wait_recv()
            total = total + back[way, j].astype(jnp.float32)
        out[at, :] = total.astype(jnp.bfloat16)

    for way in range(2):
        for j in range(n - 1):
            outward(way, j).wait_send()
            if has_share(way, j):
                share(way, j // 2).wait_send()
            backward(way, j).wait_send()


def fused(n, attn_part, resid, norm_gain, routes, gate_codes, w_gate, w_up, w_down):
    tok, width = resid.shape
    ff = w_gate.shape[2]
    vmem = pl.BlockSpec(memory_space=pltpu.VMEM)
    hbm = pl.BlockSpec(memory_space=pltpu.HBM)
    most = max(count for _, count, _ in groups_of(n))
    dma = pltpu.SemaphoreType.DMA
    return pl.pallas_call(
        functools.partial(ring_kernel, n),
        out_shape=jax.ShapeDtypeStruct((tok, width), jnp.bfloat16),
        in_specs=[vmem] * 5 + [hbm] * 3,
        out_specs=vmem,
        scratch_shapes=[
            pltpu.VMEM((n * tok, width), jnp.bfloat16),
            pltpu.VMEM((n * tok, width), jnp.bfloat16),
            pltpu.VMEM((2, n - 1, tok // 2, width), jnp.bfloat16),
            pltpu.VMEM((n, -(-n // 16) * 16, LANES), jnp.bfloat16),
            pltpu.VMEM((n * tok, LANES), jnp.float32),
            pltpu.VMEM((most * tok, ff), jnp.bfloat16),
            pltpu.VMEM((width, ff), jnp.bfloat16),
            pltpu.VMEM((width, ff), jnp.bfloat16),
            pltpu.VMEM((ff, width), jnp.bfloat16),
            dma((2, n - 1)),
            dma((2, n - 1)),
            dma((2, n // 2)),
            dma((2, n // 2)),
            dma((2, n - 1)),
            dma((2, n - 1)),
            dma((3,)),
        ],
        compiler_params=pltpu.CompilerParams(
            collective_id=0, has_side_effects=True, vmem_limit_bytes=60 * 1024 * 1024
        ),
        cost_estimate=pl.CostEstimate(
            flops=6 * n * tok * width * ff,
            bytes_accessed=6 * width * ff + 6 * tok * width,
            transcendentals=n * tok * ff,
        ),
    )(attn_part, resid, norm_gain.reshape(1, width), routes, gate_codes, w_gate, w_up, w_down)


def expert_output(hidden, w_down):
    partial_out = jnp.einsum("sekf,efd->sekd", hidden, w_down, preferred_element_type=jnp.float32)
    return lax.all_to_all(
        partial_out.astype(jnp.bfloat16), "expert", split_axis=0, concat_axis=0, tiled=True
    )


def per_device(attn_part, resid, norm_gain, routes, gate_codes, w_gate, w_up, w_down):
    tok_count = routes.shape[0]
    top_count = routes.shape[1]
    n_expert = lax.axis_size("expert")
    local_experts = w_gate.shape[0]
    fits = tok_count == 64 and local_experts == 1 and n_expert == 16
    even = w_gate.shape[2] % UP_COLS == 0 and w_down.shape[2] % DOWN_COLS == 0
    if lax.axis_size("tensor") == 1 and fits and even:
        return fused(
            n_expert, attn_part, resid, norm_gain, routes, gate_codes, w_gate, w_up, w_down
        )
    experts_all = n_expert * local_experts
    capacity = min(tok_count, 3 * tok_count * top_count // experts_all)
    flat_routes = routes.reshape(-1)
    onehot = (flat_routes[:, None] == jnp.arange(experts_all, dtype=jnp.int32)[None, :]).astype(
        jnp.int32
    )
    ranks = jnp.cumsum(onehot, axis=0) - onehot
    slot_of = jnp.sum(ranks * onehot, axis=1)
    target = flat_routes * capacity + slot_of
    tok_index = jnp.arange(tok_count * top_count, dtype=jnp.int32) // top_count
    codes = gate_codes.astype(jnp.float32)
    weights = (codes / jnp.sum(codes, axis=1, keepdims=True)).reshape(-1)
    head_total = lax.psum(attn_part[0].astype(jnp.float32).astype(jnp.bfloat16), "tensor").astype(
        jnp.float32
    )
    stream = resid.astype(jnp.float32) + head_total
    mean_sq = jnp.mean(stream * stream, axis=1, keepdims=True)
    normed = (stream * lax.rsqrt(mean_sq + 1e-06) * norm_gain.astype(jnp.float32)).astype(
        jnp.bfloat16
    )
    cols = normed.shape[1]
    buffer = jnp.zeros((experts_all * capacity, cols), jnp.bfloat16)
    buffer = buffer.at[target].set(normed[tok_index])
    outgoing = buffer.reshape(n_expert, local_experts, capacity, cols)
    received = lax.all_to_all(outgoing, "expert", split_axis=0, concat_axis=0, tiled=True)
    gate = jnp.einsum("sekd,edf->sekf", received, w_gate, preferred_element_type=jnp.float32)
    up = jnp.einsum("sekd,edf->sekf", received, w_up, preferred_element_type=jnp.float32)
    hidden = (jax.nn.silu(gate) * up).astype(jnp.bfloat16)
    returned = expert_output(hidden, w_down)
    out_cols = returned.shape[3]
    picked = returned.reshape(experts_all * capacity, out_cols)[target]
    weighted = picked.astype(jnp.float32) * weights[:, None]
    combined = jnp.sum(weighted.reshape(tok_count, top_count, out_cols), axis=1)
    return lax.psum_scatter(
        combined.astype(jnp.bfloat16), "tensor", scatter_dimension=1, tiled=True
    )


def solution(mesh):
    return jax.shard_map(
        per_device,
        mesh=mesh,
        in_specs=(
            P("tensor", ("groups", "expert"), None),
            P(("groups", "expert"), None),
            P(),
            P(("groups", "expert"), None),
            P(("groups", "expert"), None),
            P("expert", None, "tensor"),
            P("expert", None, "tensor"),
            P("expert", "tensor", None),
        ),
        out_specs=P(("groups", "expert"), "tensor"),
        check_vma=False,
    )
```

```python
import functools

import jax
import jax.numpy as jnp
from jax import lax
from jax.experimental import pallas as pl
from jax.experimental.pallas import tpu as pltpu
from jax.sharding import PartitionSpec as P

UP_COLS = 256
DOWN_COLS = 512
LANES = 128


def ring_place(index, n):
    depth = n // 4
    core, x, z = index % 2, (index // 2) % 2, index // 4
    return 2 * (z + x * (2 * depth - 1 - 2 * z)) + core


def ring_index(place, n):
    depth = n // 4
    core, q = place % 2, place // 2
    x = q // depth
    z = q + x * (2 * depth - 1 - 2 * q)
    return (z * 2 + x) * 2 + core


def left_slot(d):
    return max(2 * d - 1, 0)


def right_slot(d, n):
    return n - 1 if d == n // 2 else 2 * d


def return_order(n):
    far = n // 2
    order = [(far, 0), (far - 1, 1), (far - 1, 0)]
    for d in range(far - 2, 0, -1):
        order += [(d, 1), (d, 0)]
    return order


def groups_of(n):
    found = [(left_slot(d), 4, 2 * d + 1) for d in range(1, n // 2 - 2, 2)]
    found.append((n - 3, 3, n - 2))
    return found


def ring_kernel(
    n, attn, resid, gain, routes, codes, w_gate, w_up, w_down, out,
    rows, parts, back, shares, scale, hidden, v_gate, v_up, v_down,
    out_send, out_recv, share_send, share_recv, back_send, back_recv, load_sem,
):
    me = lax.axis_index("expert")
    place = ring_place(me, n)
    right = ring_index((place + 1) % n, n)
    left = ring_index((place + n - 1) % n, n)
    ways = ({"expert": right}, {"expert": left})
    tok = resid.shape[0]
    half = tok // 2
    experts_pad = shares.shape[1]

    barrier = pltpu.get_barrier_semaphore()
    for way in ways:
        pl.semaphore_signal(barrier, inc=1, device_id=way, device_id_type=pl.DeviceIdType.MESH)

    loads = [
        pltpu.make_async_copy(w_gate.at[0], v_gate, load_sem.at[0]),
        pltpu.make_async_copy(w_up.at[0], v_up, load_sem.at[1]),
        pltpu.make_async_copy(w_down.at[0], v_down, load_sem.at[2]),
    ]
    for load in loads:
        load.start()

    def norm(first, count):
        at = pl.ds(first, count)
        stream = resid[at, :].astype(jnp.float32) + attn[0, at, :].astype(jnp.float32)
        mean_sq = jnp.mean(stream * stream, axis=1, keepdims=True)
        scaled = stream * lax.rsqrt(mean_sq + 1e-06) * gain[...].astype(jnp.float32).reshape(1, -1)
        rows[at, :] = scaled.astype(jnp.bfloat16)

    for first in range(0, tok, 16):
        norm(first, 16)

    pl.semaphore_wait(barrier, 2)

    def piece(slot, which):
        return pl.ds(slot * tok + which * half, half)

    def slot_of(way, d):
        return left_slot(d) if way == 0 else right_slot(d, n)

    def outward(way, j):
        d, which = j // 2, (j % 2 if way == 0 else 1 - j % 2)
        here, there = slot_of(way, d), slot_of(way, d + 1)
        return pltpu.make_async_remote_copy(
            rows.at[piece(here, which)], rows.at[piece(there, which)],
            out_send.at[way, j], out_recv.at[way, j],
            device_id=ways[way], device_id_type=pl.DeviceIdType.MESH,
        )

    def share(way, d):
        return pltpu.make_async_remote_copy(
            shares.at[slot_of(way, d)], shares.at[slot_of(way, d + 1)],
            share_send.at[way, d], share_recv.at[way, d],
            device_id=ways[way], device_id_type=pl.DeviceIdType.MESH,
        )

    def has_share(way, j):
        return j % 2 == 0 and not (way == 1 and j // 2 == n // 2 - 1)

    def send_out(way, j):
        outward(way, j).start()
        if j > 0 and has_share(way, j):
            share(way, j // 2).start()

    def arrive(j):
        for way in range(2):
            outward(way, j).wait_recv()
            if has_share(way, j):
                share(way, j // 2).wait_recv()
            if j + 2 < n - 1:
                send_out(way, j + 2)

    for j in range(2):
        for way in range(2):
            send_out(way, j)

    code = codes[...].astype(jnp.float32)
    weight = code / jnp.sum(code, axis=0, keepdims=True)
    expert = lax.broadcasted_iota(jnp.int32, (experts_pad, tok), 0)
    dense = jnp.zeros((experts_pad, tok), jnp.float32)
    for k in range(routes.shape[0]):
        dense = dense + jnp.where(expert == routes[k:k + 1, :], weight[k:k + 1, :], 0.0)
    high = dense.astype(jnp.bfloat16)
    low = (dense - high.astype(jnp.float32)).astype(jnp.bfloat16)
    shares[0] = jnp.concatenate([high, low], axis=1)
    for way in range(2):
        share(way, 0).start()

    pick = (lax.broadcasted_iota(jnp.int32, (experts_pad, LANES), 0) == me).astype(jnp.bfloat16)

    def prepare(first, count):
        for slot in range(first, first + count):
            wide = lax.dot_general(
                shares[slot], pick, (((0,), (0,)), ((), ())), preferred_element_type=jnp.float32
            )
            scale[pl.ds(slot * tok, tok), :] = wide[:tok] + wide[tok:]

    def up_step(first, count, c):
        at = pl.ds(first * tok, count * tok)
        cols = pl.ds(pl.multiple_of(c * UP_COLS, UP_COLS), UP_COLS)
        x = rows[at, :]
        gate = jnp.dot(x, v_gate[:, cols], preferred_element_type=jnp.float32)
        up = jnp.dot(x, v_up[:, cols], preferred_element_type=jnp.float32)
        factor = jnp.concatenate([scale[at, :]] * (UP_COLS // LANES), axis=1)
        value = gate / (1.0 + jnp.exp(-gate)) * up * factor
        hidden[pl.ds(0, count * tok), cols] = value.astype(jnp.bfloat16)

    def down_step(first, count, c):
        cols = pl.ds(pl.multiple_of(c * DOWN_COLS, DOWN_COLS), DOWN_COLS)
        total = jnp.dot(
            hidden[pl.ds(0, count * tok), :], v_down[:, cols], preferred_element_type=jnp.float32
        )
        parts[pl.ds(first * tok, count * tok), cols] = total.astype(jnp.bfloat16)

    up_steps = v_gate.shape[1] // UP_COLS
    down_steps = v_down.shape[1] // DOWN_COLS
    up_cost = 2 * v_gate.shape[0] * UP_COLS
    down_cost = v_down.shape[0] * DOWN_COLS
    whole_cost = up_steps * up_cost + down_steps * down_cost

    def multiply(first, count, begin, end):
        def inside(done, cost):
            return begin <= (done + cost / 2) / whole_cost < end

        ups = [c for c in range(up_steps) if inside(c * up_cost, up_cost)]
        downs = [c for c in range(down_steps) if inside(up_steps * up_cost + c * down_cost, down_cost)]
        if ups:
            @pl.loop(ups[0], ups[-1] + 1)
            def _(c):
                up_step(first, count, c)
        if downs:
            @pl.loop(downs[0], downs[-1] + 1)
            def _(c):
                down_step(first, count, c)

    orders = return_order(n)

    def backward(way, j):
        d, which = orders[j]
        which = which if way == 0 else 1 - which
        slot = slot_of(1 - way, d)
        return pltpu.make_async_remote_copy(
            parts.at[piece(slot, which)], back.at[way, j],
            back_send.at[way, j], back_recv.at[way, j],
            device_id=ways[way], device_id_type=pl.DeviceIdType.MESH,
        )

    def send_back(way, j):
        d, which = orders[j]
        if (d + 1, which) in orders:
            earlier = orders.index((d + 1, which))
            backward(way, earlier).wait_recv()
            at = piece(slot_of(1 - way, d), which if way == 0 else 1 - which)
            total = parts[at, :].astype(jnp.float32) + back[way, earlier].astype(jnp.float32)
            parts[at, :] = total.astype(jnp.bfloat16)
        backward(way, j).start()

    plan = groups_of(n)
    arrived = -1
    for g, (first, count, needed) in enumerate(plan):
        while arrived < needed:
            arrived += 1
            arrive(arrived)
        if g == 0:
            for load in loads:
                load.wait()
        prepare(first, count)
        later = plan[g + 1][2] if g + 1 < len(plan) else arrived
        gaps = max(later - arrived, 1)
        for gap in range(gaps):
            multiply(first, count, gap / gaps, (gap + 1) / gaps if gap + 1 < gaps else 2.0)
            if gap + 1 < gaps:
                arrived += 1
                arrive(arrived)

    prepare(0, 1)
    spread = n - 5
    for j in range(n - 1):
        for way in range(2):
            send_back(way, j)
        if 1 <= j <= spread:
            multiply(0, 1, (j - 1) / spread, j / spread if j < spread else 2.0)

    for k in range(2):
        which = 1 - k
        at = pl.ds(which * half, half)
        total = parts[at, :].astype(jnp.float32)
        for way in range(2):
            j = orders.index((1, which if way == 0 else 1 - which))
            backward(way, j).wait_recv()
            total = total + back[way, j].astype(jnp.float32)
        out[at, :] = total.astype(jnp.bfloat16)

    for way in range(2):
        for j in range(n - 1):
            outward(way, j).wait_send()
            if has_share(way, j):
                share(way, j // 2).wait_send()
            backward(way, j).wait_send()


def fused(n, attn_part, resid, norm_gain, routes, gate_codes, w_gate, w_up, w_down):
    tok, width = resid.shape
    ff = w_gate.shape[2]
    vmem = pl.BlockSpec(memory_space=pltpu.VMEM)
    hbm = pl.BlockSpec(memory_space=pltpu.HBM)
    most = max(count for _, count, _ in groups_of(n))
    dma = pltpu.SemaphoreType.DMA
    return pl.pallas_call(
        functools.partial(ring_kernel, n),
        out_shape=jax.ShapeDtypeStruct((tok, width), jnp.bfloat16),
        in_specs=[vmem] * 5 + [hbm] * 3,
        out_specs=vmem,
        scratch_shapes=[
            pltpu.VMEM((n * tok, width), jnp.bfloat16),
            pltpu.VMEM((n * tok, width), jnp.bfloat16),
            pltpu.VMEM((2, n - 1, tok // 2, width), jnp.bfloat16),
            pltpu.VMEM((n, -(-n // 16) * 16, LANES), jnp.bfloat16),
            pltpu.VMEM((n * tok, LANES), jnp.float32),
            pltpu.VMEM((most * tok, ff), jnp.bfloat16),
            pltpu.VMEM((width, ff), jnp.bfloat16),
            pltpu.VMEM((width, ff), jnp.bfloat16),
            pltpu.VMEM((ff, width), jnp.bfloat16),
            dma((2, n - 1)),
            dma((2, n - 1)),
            dma((2, n // 2)),
            dma((2, n // 2)),
            dma((2, n - 1)),
            dma((2, n - 1)),
            dma((3,)),
        ],
        compiler_params=pltpu.CompilerParams(
            collective_id=0, has_side_effects=True, vmem_limit_bytes=60 * 1024 * 1024
        ),
        cost_estimate=pl.CostEstimate(
            flops=6 * n * tok * width * ff,
            bytes_accessed=6 * width * ff + 6 * tok * width,
            transcendentals=n * tok * ff,
        ),
    )(attn_part, resid, norm_gain, routes.T, gate_codes.T, w_gate, w_up, w_down)


def expert_output(hidden, w_down):
    partial_out = jnp.einsum("sekf,efd->sekd", hidden, w_down, preferred_element_type=jnp.float32)
    return lax.all_to_all(
        partial_out.astype(jnp.bfloat16), "expert", split_axis=0, concat_axis=0, tiled=True
    )


def per_device(attn_part, resid, norm_gain, routes, gate_codes, w_gate, w_up, w_down):
    tok_count = routes.shape[0]
    top_count = routes.shape[1]
    n_expert = lax.axis_size("expert")
    local_experts = w_gate.shape[0]
    fits = tok_count == 64 and local_experts == 1 and n_expert == 16
    even = w_gate.shape[2] % UP_COLS == 0 and w_down.shape[2] % DOWN_COLS == 0
    if lax.axis_size("tensor") == 1 and fits and even:
        return fused(
            n_expert, attn_part, resid, norm_gain, routes, gate_codes, w_gate, w_up, w_down
        )
    experts_all = n_expert * local_experts
    capacity = min(tok_count, 3 * tok_count * top_count // experts_all)
    flat_routes = routes.reshape(-1)
    onehot = (flat_routes[:, None] == jnp.arange(experts_all, dtype=jnp.int32)[None, :]).astype(
        jnp.int32
    )
    ranks = jnp.cumsum(onehot, axis=0) - onehot
    slot_of = jnp.sum(ranks * onehot, axis=1)
    target = flat_routes * capacity + slot_of
    tok_index = jnp.arange(tok_count * top_count, dtype=jnp.int32) // top_count
    codes = gate_codes.astype(jnp.float32)
    weights = (codes / jnp.sum(codes, axis=1, keepdims=True)).reshape(-1)
    head_total = lax.psum(attn_part[0].astype(jnp.float32).astype(jnp.bfloat16), "tensor").astype(
        jnp.float32
    )
    stream = resid.astype(jnp.float32) + head_total
    mean_sq = jnp.mean(stream * stream, axis=1, keepdims=True)
    normed = (stream * lax.rsqrt(mean_sq + 1e-06) * norm_gain.astype(jnp.float32)).astype(
        jnp.bfloat16
    )
    cols = normed.shape[1]
    buffer = jnp.zeros((experts_all * capacity, cols), jnp.bfloat16)
    buffer = buffer.at[target].set(normed[tok_index])
    outgoing = buffer.reshape(n_expert, local_experts, capacity, cols)
    received = lax.all_to_all(outgoing, "expert", split_axis=0, concat_axis=0, tiled=True)
    gate = jnp.einsum("sekd,edf->sekf", received, w_gate, preferred_element_type=jnp.float32)
    up = jnp.einsum("sekd,edf->sekf", received, w_up, preferred_element_type=jnp.float32)
    hidden = (jax.nn.silu(gate) * up).astype(jnp.bfloat16)
    returned = expert_output(hidden, w_down)
    out_cols = returned.shape[3]
    picked = returned.reshape(experts_all * capacity, out_cols)[target]
    weighted = picked.astype(jnp.float32) * weights[:, None]
    combined = jnp.sum(weighted.reshape(tok_count, top_count, out_cols), axis=1)
    return lax.psum_scatter(
        combined.astype(jnp.bfloat16), "tensor", scatter_dimension=1, tiled=True
    )


def solution(mesh):
    return jax.shard_map(
        per_device,
        mesh=mesh,
        in_specs=(
            P("tensor", ("groups", "expert"), None),
            P(("groups", "expert"), None),
            P(),
            P(("groups", "expert"), None),
            P(("groups", "expert"), None),
            P("expert", None, "tensor"),
            P("expert", None, "tensor"),
            P("expert", "tensor", None),
        ),
        out_specs=P(("groups", "expert"), "tensor"),
        check_vma=False,
    )
```
